32 devices in a mesh: lat: 4 (over y, x), lon: 2 (over core), ens: 4 (over z).
Axes of the slice: x: 2, y: 2, z: 4, core: 2. Of those that a mesh axis runs over, the one named last changes fastest.
Arguments:
- inputs: bfloat16 [4, 8, 1440, 256], P('ens', 'lat', 'lon'), may hold values from -12 to 12
- weight: bfloat16 [9, 256, 256], replicated, may hold values from -0.125 to 0.125
- spread: int32 [8], P('lat'), may hold values from 2 to 16, as said below
- target: bfloat16 [8, 1440, 256], P('lat', 'lon'), may hold values from -6 to 6
Outputs:
- response: bfloat16 [4, 8, 1440, 256], P('ens', 'lat', 'lon')
- grad_input: bfloat16 [4, 8, 1440, 256], P('ens', 'lat', 'lon')
- grad_weight: float32 [9, 256, 256], replicated
- loss: float32 [], replicated
The draws below stay inside these ranges and needn't reach their ends.
Inputs may be any that keep to these rules, and one draw needn't show every extreme that they name: The filter of row o spans 2 spread[o] + 1 longitudes; spread is 16 on the 2 polar rows at each pole, which ignore it, and on the next row toward the equator.
All inputs are finite; a program needn't handle non-finite values.
Results may differ from the reference program's by a relative error of at most 0.009.
Values may be sent and summed in bfloat16 or wider, within the bound.
A program may use at most 128 MiB of HBM per device.

```python
import math
import jax
import jax.numpy as jnp
from jax import lax

C = 256
K = 9
PCAP = 2
HMAX = 16
LON_DEV = 720
E = 4
NLAT = 8
NLON = 1440


def draw_inputs(key, part):
    keys = jax.random.split(key, 4)
    shape = (E, NLAT, NLON, C)
    rough = jax.random.normal(keys[0], shape, jnp.float32)
    level = jax.random.normal(keys[1], (E, NLAT, 1, C), jnp.float32)
    amplitude = jax.random.normal(keys[2], (E, NLAT, 1, C), jnp.float32)
    phase = jax.random.uniform(keys[3], (E, NLAT, 1, C), jnp.float32, 0.0, 2.0 * math.pi)
    angles = 2.0 * math.pi * jnp.arange(NLON).astype(jnp.float32) / NLON
    lat_rows = jnp.arange(NLAT).astype(jnp.int32)
    distance = jnp.minimum(lat_rows, NLAT - 1 - lat_rows)
    cap_rows = (distance < PCAP - 1).astype(jnp.float32)[None, :, None, None]
    smooth = level + amplitude * jnp.cos(angles[None, None, :, None] - phase)
    field = rough + cap_rows * smooth
    return jnp.clip(field, -12.0, 12.0).astype(jnp.bfloat16)


def draw_spread(key, part):
    lat_rows = jnp.arange(NLAT).astype(jnp.int32)
    distance = jnp.minimum(lat_rows, NLAT - 1 - lat_rows)
    halfway = NLAT // 2
    baseline = 2 + (HMAX - 2) * (halfway - 1 - distance) // max(halfway - 1, 1)
    jitter = jax.random.randint(key, (NLAT,), 0, HMAX // 2 + 1)
    values = jnp.clip(baseline + jitter, 2, HMAX)
    values = jnp.where(lat_rows == halfway - 1, 2, values)
    values = jnp.where(distance <= PCAP, HMAX, values)
    return values.astype(jnp.int32)


def shard_levels(key, dims, cuts, smallest, largest):
    factor_of, own = 1.0, jax.random.fold_in(key, 6)
    for axis_at, parts in cuts:
        heights = jnp.exp(jax.random.uniform(jax.random.fold_in(own, axis_at), (parts,), jnp.float32, smallest / len(cuts), largest / len(cuts)))
        factor_of = factor_of * jnp.repeat(heights, dims[axis_at] // parts).reshape([-1 if axis == axis_at else 1 for axis in range(len(dims))])
    return factor_of


def scatter_about(rng, dims, scale, bound, cuts=(), kind=jnp.bfloat16):
    factor_of = shard_levels(rng, dims, cuts, -0.22, 0.18) if cuts else 1.0
    drawn = jax.random.normal(rng, dims, jnp.float32) * scale * factor_of
    return jnp.minimum(jnp.maximum(drawn, -bound), bound).astype(kind)


def setup_inputs(seed: int = 0) -> dict:
    seeds = jax.random.split(jax.random.key(seed), 5)
    inputs = draw_inputs(jax.random.fold_in(seeds[4], 71), 0)
    weight = scatter_about(seeds[1], (K, C, C), (K * C) ** -0.5, 0.125)
    spread = draw_spread(jax.random.fold_in(seeds[4], 71), 0)
    target = scatter_about(seeds[3], (NLAT, NLON, C), 1.0, 6.0, ((0, 4), (1, 2)))
    return dict(inputs=inputs, weight=weight, spread=spread, target=target)


highest = lax.Precision.HIGHEST

def kernel_rows(spread_rows, lon_count, reach):
    halves = spread_rows.astype(jnp.float32)[:, None, None, None] / 2.0
    columns = jnp.arange(lon_count)
    window_cols = jnp.arange(lon_count + 2 * reach)
    offsets = (window_cols[None, :] - reach - columns[:, None]).astype(jnp.float32)
    centres = (jnp.arange(3) - 1).astype(jnp.float32)[None, :, None, None] * halves
    values = jnp.maximum(0.0, 1.0 - jnp.abs(offsets[None, None] - centres) / halves) / halves
    return values.astype(jnp.bfloat16)

def circle_basis(first_col, lon_count, circle):
    angles = 2.0 * math.pi * (first_col + jnp.arange(lon_count)).astype(jnp.float32) / circle
    return jnp.stack([jnp.ones_like(angles), jnp.cos(angles), jnp.sin(angles)])

def circular(circle_sums, basis, circle, row_count):
    cos_wave = basis[1][None, None, :, None]
    sin_wave = basis[2][None, None, :, None]
    pieces = []
    for lat_tap in range(3):
        tap_sums = circle_sums[:, :, lat_tap:lat_tap + row_count]
        mean_part = tap_sums[:, 0][:, :, None, :] / circle
        cosine_part = 2.0 / circle * (cos_wave * tap_sums[:, 1][:, :, None, :] + sin_wave * tap_sums[:, 2][:, :, None, :])
        sine_part = 2.0 / circle * (cos_wave * tap_sums[:, 2][:, :, None, :] - sin_wave * tap_sums[:, 1][:, :, None, :])
        pieces += [jnp.broadcast_to(mean_part, cosine_part.shape), cosine_part, sine_part]
    return jnp.stack(pieces, 2)

def reference(inputs, weight, spread, target):
    members = inputs.shape[0]
    reach = HMAX
    padded = jnp.pad(inputs, ((0, 0), (1, 1), (0, 0), (0, 0)))
    padded = jnp.concatenate([padded[:, :, NLON - reach:], padded, padded[:, :, :reach]], 2)
    kernels = kernel_rows(spread, LON_DEV, reach).astype(jnp.float32)
    basis = circle_basis(0, NLON, NLON)
    lat_rows = jnp.arange(NLAT).astype(jnp.int32)
    polar_flags = (lat_rows < PCAP) | (lat_rows >= NLAT - PCAP)
    weight_wide = weight.astype(jnp.float32)

    def convolve(window_rows, kernel, flag):
        blocks = jnp.stack([window_rows[:, :, block_start:block_start + LON_DEV + 2 * reach] for block_start in range(0, NLON, LON_DEV)])
        banded = jnp.einsum('bjq,nerqc->erbnjc', kernel, blocks)
        banded = banded.reshape(members, K, NLON, C)
        centre = window_rows[:, :, reach:reach + NLON]
        circle_sums = jnp.einsum('pj,erjc->eprc', basis, centre, precision=highest)
        rounds = circular(circle_sums, basis, NLON, 1)[:, 0]
        return jnp.where(flag, rounds, banded)

    def forward_row(items):
        row_index, kernel, flag = items
        window_rows = lax.dynamic_slice_in_dim(padded, row_index, 3, 1).astype(jnp.float32)
        features = convolve(window_rows, kernel, flag).astype(jnp.bfloat16)
        return jnp.einsum('ekjc,kcd->ejd', features.astype(jnp.float32), weight_wide).astype(jnp.bfloat16)
    response = lax.map(forward_row, (lat_rows, kernels, polar_flags)).transpose(1, 0, 2, 3)
    values = response.astype(jnp.float32)
    truth = target.astype(jnp.float32)[None]
    miss = values - truth
    own_dist = jnp.sqrt(miss * miss + 0.25)
    own_slope = miss / own_dist
    pair_dist = jnp.zeros_like(values)
    pair_slope = jnp.zeros_like(values)
    for member in range(members):
        gap_value = values - values[member][None]
        distance = jnp.sqrt(gap_value * gap_value + 0.25)
        pair_dist = pair_dist + distance
        pair_slope = pair_slope + gap_value / distance
    pair_dist = pair_dist - 0.5
    lat_weight = jnp.sin(math.pi * (lat_rows.astype(jnp.float32) + 0.5) / NLAT)[None, :, None, None]
    scores = own_dist / members - pair_dist / (2 * members * (members - 1))
    loss = jnp.sum(lat_weight * scores) / (NLAT * NLON * C)
    slopes = (lat_weight * (own_slope / members - pair_slope / (members * (members - 1)))).astype(jnp.bfloat16)

    def backward_row(carry, items):
        grad_w, grad_x = carry
        row_index, kernel, flag, row_slopes = items
        window_rows = lax.dynamic_slice_in_dim(padded, row_index, 3, 1).astype(jnp.float32)
        features, pull_back = jax.vjp(lambda rows_in: convolve(rows_in, kernel, flag), window_rows)
        features = lax.optimization_barrier(features.astype(jnp.bfloat16)).astype(jnp.float32)
        slopes_wide = row_slopes.astype(jnp.float32)
        grad_w = grad_w + jnp.einsum('ekjc,ejd->kcd', features, slopes_wide)
        feature_grad = jnp.einsum('ejd,kcd->ekjc', slopes_wide, weight_wide)
        feature_grad = lax.optimization_barrier(feature_grad.astype(jnp.bfloat16)).astype(jnp.float32)
        row_grad, = pull_back(feature_grad)
        current = lax.dynamic_slice_in_dim(grad_x, row_index, 3, 1)
        grad_x = lax.dynamic_update_slice_in_dim(grad_x, current + row_grad, row_index, 1)
        return ((grad_w, grad_x), None)
    start_carry = (jnp.zeros((K, C, C), jnp.float32), jnp.zeros(padded.shape, jnp.float32))
    (grad_w, grad_x), _ = lax.scan(backward_row, start_carry, (lat_rows, kernels, polar_flags, slopes.transpose(1, 0, 2, 3)))
    core = grad_x[:, 1:NLAT + 1]
    inner = core[:, :, reach:reach + NLON]
    inner = inner.at[:, :, NLON - reach:].add(core[:, :, :reach])
    inner = inner.at[:, :, :reach].add(core[:, :, reach + NLON:])
    grad_weight = grad_w * math.sqrt(K * C) / (NLAT * NLON)
    return (response, inner.astype(jnp.bfloat16), grad_weight, loss)
```

```python
import functools
import math

import jax
import jax.numpy as jnp
from jax import lax
from jax.experimental import pallas as pl
from jax.experimental.pallas import tpu as pltpu
from jax.sharding import PartitionSpec as P

PCAP = 2
HMAX = 16


highest = lax.Precision.HIGHEST


def extended_2(block, sides, width, periodic):
    for axis, dim in sides:
        count = lax.axis_size(axis)
        forward = [(i, i + 1) for i in range(count - 1)]
        if periodic:
            forward.append((count - 1, 0))
        backward = [(target, source) for source, target in forward]
        low = lax.ppermute(
            lax.slice_in_dim(block, block.shape[dim] - width, None, axis=dim), axis, forward
        )
        high = lax.ppermute(lax.slice_in_dim(block, 0, width, axis=dim), axis, backward)
        block = jnp.concatenate([low, block, high], axis=dim)
    return block


def kernel_rows(spread_rows, lon_count, reach):
    halves = spread_rows.astype(jnp.float32)[:, None, None, None] / 2.0
    columns = jnp.arange(lon_count)
    window_cols = jnp.arange(lon_count + 2 * reach)
    offsets = (window_cols[None, :] - reach - columns[:, None]).astype(jnp.float32)
    centres = (jnp.arange(3) - 1).astype(jnp.float32)[None, :, None, None] * halves
    values = jnp.maximum(0.0, 1.0 - jnp.abs(offsets[None, None] - centres) / halves) / halves
    return values.astype(jnp.bfloat16)


def circle_basis(first_col, lon_count, circle):
    angles = 2.0 * math.pi * (first_col + jnp.arange(lon_count)).astype(jnp.float32) / circle
    return jnp.stack([jnp.ones_like(angles), jnp.cos(angles), jnp.sin(angles)])


def circular(circle_sums, basis, circle, row_count):
    cos_wave = basis[1][None, None, :, None]
    sin_wave = basis[2][None, None, :, None]
    pieces = []
    for lat_tap in range(3):
        tap_sums = circle_sums[:, :, lat_tap : lat_tap + row_count]
        mean_part = tap_sums[:, 0][:, :, None, :] / circle
        cosine_part = (
            2.0
            / circle
            * (cos_wave * tap_sums[:, 1][:, :, None, :] + sin_wave * tap_sums[:, 2][:, :, None, :])
        )
        sine_part = (
            2.0
            / circle
            * (cos_wave * tap_sums[:, 2][:, :, None, :] - sin_wave * tap_sums[:, 1][:, :, None, :])
        )
        pieces += [jnp.broadcast_to(mean_part, cosine_part.shape), cosine_part, sine_part]
    return jnp.stack(pieces, 2)


def crps_terms(values, every_member, truth, lat_weight, member_total):
    miss = values - truth
    own_dist = jnp.sqrt(miss * miss + 0.25)
    own_slope = miss / own_dist

    def add_member(member, carry):
        pair_dist, pair_slope = carry
        other = lax.dynamic_index_in_dim(every_member, member, 0, keepdims=True).astype(jnp.float32)
        gap_value = values - other
        distance = jnp.sqrt(gap_value * gap_value + 0.25)
        return (pair_dist + distance, pair_slope + gap_value / distance)

    start = (jnp.zeros_like(values), jnp.zeros_like(values))
    pair_dist, pair_slope = lax.fori_loop(0, member_total, add_member, start)
    pair_dist = pair_dist - 0.5
    scores = own_dist / member_total - pair_dist / (2 * member_total * (member_total - 1))
    weighted = jnp.sum(lat_weight * scores)
    slopes = (
        lat_weight * (own_slope / member_total - pair_slope / (member_total * (member_total - 1)))
    ).astype(jnp.bfloat16)
    return (weighted, slopes)


MESH = pl.DeviceIdType.MESH
ROWDOT = (((0,), (0,)), ((), ()))
COLDOT = (((1,), (1,)), ((), ()))


def pick_tile(lon_count):
    for tile in (240, 144, 96, 80, 48, 32, 16):
        if lon_count % tile == 0:
            return tile
    return 0


def fits(row_count, lon_count, channels, taps):
    lats, lons, members = (lax.axis_size(a) for a in ("lat", "lon", "ens"))
    return (
        lons == 2
        and members <= 8
        and lats <= 8
        and channels % 256 == 0
        and pick_tile(lon_count) > 0
        and (taps * channels) % (16 * lats * members) == 0
    )


def middle(scale, feat, weight, target, row_weight, resp, fg, grad_w, loss, rsp, gath, acc, losses,
           send1, recv1, out2, in2, red2, out3, in3, red3, full, sems, loss_sems):
    members, lats = lax.axis_size("ens"), lax.axis_size("lat")
    me, my_lat, my_lon = lax.axis_index("ens"), lax.axis_index("lat"), lax.axis_index("lon")
    rows, taps, lon_count, channels = feat.shape
    tile = pick_tile(lon_count)
    per_row = lon_count // tile
    chunks = rows * per_row
    half = channels // 2

    def peer(axis, here, count, step):
        return {axis: lax.rem(here + step, count)}

    barrier = pltpu.get_barrier_semaphore()
    peers = (
        [peer("ens", me, members, p) for p in range(1, members)]
        + [peer("lat", my_lat, lats, p) for p in range(1, lats)]
        + [{"lon": 1 - my_lon}]
    )
    for other in peers:
        pl.semaphore_signal(barrier, inc=1, device_id=other, device_id_type=MESH)
    pl.semaphore_wait(barrier, len(peers))

    def where(i):
        return i // per_row, pl.ds(pl.multiple_of(lax.rem(i, per_row) * tile, 16), tile)

    def gather_copy(i, p):
        o, cols = where(i)
        return pltpu.make_async_remote_copy(
            src_ref=rsp.at[o, cols], dst_ref=gath.at[p - 1, o, cols],
            send_sem=send1.at[p - 1, i], recv_sem=recv1.at[p - 1, i],
            device_id=peer("ens", me, members, p), device_id_type=MESH,
        )

    def forward(i, carry):
        o, cols = where(i)
        total = jnp.zeros((tile, channels), jnp.float32)
        for k in range(taps):
            total = total + jnp.dot(feat[o, k, cols], weight[k], preferred_element_type=jnp.float32)
        rsp[o, cols] = total.astype(jnp.bfloat16)
        for p in range(1, members):
            gather_copy(i, p).start()
        return carry

    lax.fori_loop(0, chunks, forward, 0)
    resp[...] = rsp[...]
    acc[...] = jnp.zeros_like(acc)

    def backward(i, carry):
        o, cols = where(i)
        for p in range(1, members):
            gather_copy(i, p).wait_recv()
        value = rsp[o, cols].astype(jnp.float32)
        miss = value - target[o, cols].astype(jnp.float32)
        square = miss * miss + 0.25
        inverse = lax.rsqrt(square)
        own_dist = square * inverse
        own_slope = miss * inverse
        pair_dist = jnp.zeros_like(value)
        pair_slope = jnp.zeros_like(value)
        for p in range(1, members):
            gap = value - gath[p - 1, o, cols].astype(jnp.float32)
            square = gap * gap + 0.25
            inverse = lax.rsqrt(square)
            pair_dist = pair_dist + square * inverse
            pair_slope = pair_slope + gap * inverse
        lat_weight = row_weight[o]
        score = own_dist / members - pair_dist / (2 * members * (members - 1))
        slope = lat_weight * (own_slope / members - pair_slope / (members * (members - 1)))
        slope = slope.astype(jnp.bfloat16)
        score = lat_weight * jnp.sum(score.reshape(tile // 8, 8, channels), axis=0)
        for k in range(taps):
            part = lax.dot_general(feat[o, k, cols], slope, ROWDOT, preferred_element_type=jnp.float32)
            for h in range(2):
                acc[h, pl.ds(k * channels, channels)] += part[:, h * half : (h + 1) * half]
            fg[o, k, cols] = lax.dot_general(
                slope, weight[k], COLDOT, preferred_element_type=jnp.float32
            ).astype(jnp.bfloat16)
        return carry + score

    score = lax.fori_loop(0, chunks, backward, jnp.zeros((8, channels), jnp.float32))
    part_loss = jnp.sum(score, axis=1, keepdims=True) * jnp.ones((8, 128), jnp.float32)

    def remote(src, dst, at, other):
        return pltpu.make_async_remote_copy(
            src_ref=src, dst_ref=dst, send_sem=sems.at[0, at], recv_sem=sems.at[1, at],
            device_id=other, device_id_type=MESH,
        )

    def remote_loss(src, dst, at, other):
        return pltpu.make_async_remote_copy(
            src_ref=src, dst_ref=dst, send_sem=loss_sems.at[0, at], recv_sem=loss_sems.at[1, at],
            device_id=other, device_id_type=MESH,
        )

    def finish(copies):
        for copy in copies:
            copy.wait_recv()

    pending = []
    at, lat_at = 0, 0
    out2[...] = acc[1 - my_lon].astype(jnp.bfloat16).reshape(out2.shape)
    losses[0] = part_loss
    copies = [
        remote(out2, in2, at, {"lon": 1 - my_lon}),
        remote_loss(losses.at[0], losses.at[1], lat_at, {"lon": 1 - my_lon}),
    ]
    for copy in copies:
        copy.start()
    finish(copies)
    pending += copies
    at, lat_at = at + 1, lat_at + 1
    red2[...] = acc[my_lon].reshape(red2.shape) + in2[...].astype(jnp.float32)
    base = 2
    losses[base + my_lat] = losses[0] + losses[1]
    send2 = out3
    send2[...] = red2[...].astype(jnp.bfloat16)
    copies = []
    for p in range(1, lats):
        other = peer("lat", my_lat, lats, p)
        copies.append(remote(send2.at[other["lat"]], in3.at[p - 1], at, other))
        copies.append(remote_loss(losses.at[base + my_lat], losses.at[base + my_lat], lat_at, other))
        at, lat_at = at + 1, lat_at + 1
    for copy in copies:
        copy.start()
    finish(copies)
    pending += copies
    total = red2[my_lat]
    for p in range(1, lats):
        total = total + in3[p - 1].astype(jnp.float32)
    parts = red3.shape[0]
    red3[...] = total.reshape(parts, total.shape[0] // parts, half)
    total = losses[base]
    for p in range(1, lats):
        total = total + losses[base + p]
    base = base + lats
    losses[base + me] = total
    red_out, red_in = full_split(full, members)
    red_out[...] = red3[...].astype(jnp.bfloat16)
    copies = []
    for p in range(1, members):
        other = peer("ens", me, members, p)
        copies.append(remote(red_out.at[other["ens"]], red_in.at[p - 1], at, other))
        copies.append(remote_loss(losses.at[base + me], losses.at[base + me], lat_at, other))
        at, lat_at = at + 1, lat_at + 1
    for copy in copies:
        copy.start()
    finish(copies)
    pending += copies
    total = red3[me]
    for p in range(1, members):
        total = total + red_in[p - 1].astype(jnp.float32)
    gathered = full[2]
    gathered[my_lon, my_lat, me] = (total * scale).astype(jnp.bfloat16)
    total = losses[base]
    for p in range(1, members):
        total = total + losses[base + p]
    loss[...] = total
    mine = gathered.at[my_lon, my_lat, me]
    copies = []
    for p in range(1, members):
        copies.append(remote(mine, mine, at, peer("ens", me, members, p)))
        at += 1
    for copy in copies:
        copy.start()
    finish(copies)
    pending += copies
    mine = gathered.at[my_lon, my_lat]
    copies = []
    for p in range(1, lats):
        copies.append(remote(mine, mine, at, peer("lat", my_lat, lats, p)))
        at += 1
    for copy in copies:
        copy.start()
    finish(copies)
    pending += copies
    mine = gathered.at[my_lon]
    copies = [remote(mine, mine, at, {"lon": 1 - my_lon})]
    copies[0].start()
    finish(copies)
    pending += copies
    for h in range(2):
        grad_w[:, :, h * half : (h + 1) * half] = (
            gathered[h].astype(jnp.float32).reshape(taps, channels, half)
        )
    for copy in pending:
        copy.wait_send()

    def drain(i, carry):
        for p in range(1, members):
            gather_copy(i, p).wait_send()
        return carry

    lax.fori_loop(0, chunks, drain, 0)


def full_split(full, members):
    return full[0], full[1]


def run_middle(scale, feat, weight, target, row_weight):
    members, lats = lax.axis_size("ens"), lax.axis_size("lat")
    rows, taps, lon_count, channels = feat.shape
    chunks = rows * (lon_count // pick_tile(lon_count))
    half = channels // 2
    flat = taps * channels
    band, piece = flat // lats, flat // lats // members
    bf16, f32 = jnp.bfloat16, jnp.float32
    shape = jax.ShapeDtypeStruct
    whole = pl.BlockSpec(memory_space=pltpu.VMEM)
    count = 1 + 2 * (lats - 1) + 2 * (members - 1) + 1
    loss_count = 1 + (lats - 1) + (members - 1)
    return pl.pallas_call(
        functools.partial(middle, scale),
        out_shape=[
            shape((rows, lon_count, channels), bf16),
            shape(feat.shape, bf16),
            shape((taps, channels, channels), f32),
            shape((8, 128), f32),
        ],
        in_specs=[whole] * 4,
        out_specs=[whole] * 4,
        scratch_shapes=[
            pltpu.VMEM((rows, lon_count, channels), bf16),
            pltpu.VMEM((members - 1, rows, lon_count, channels), bf16),
            pltpu.VMEM((2, flat, half), f32),
            pltpu.VMEM((2 + lats + members, 8, 128), f32),
            pltpu.SemaphoreType.DMA((members - 1, chunks)),
            pltpu.SemaphoreType.DMA((members - 1, chunks)),
            pltpu.VMEM((lats, band, half), bf16),
            pltpu.VMEM((lats, band, half), bf16),
            pltpu.VMEM((lats, band, half), f32),
            pltpu.VMEM((lats, band, half), bf16),
            pltpu.VMEM((lats - 1, band, half), bf16),
            pltpu.VMEM((members, piece, half), f32),
            [
                pltpu.VMEM((members, piece, half), bf16),
                pltpu.VMEM((members - 1, piece, half), bf16),
                pltpu.VMEM((2, lats, members, piece, half), bf16),
            ],
            pltpu.SemaphoreType.DMA((2, count)),
            pltpu.SemaphoreType.DMA((2, loss_count)),
        ],
        compiler_params=pltpu.CompilerParams(
            collective_id=0, has_side_effects=True, vmem_limit_bytes=50 * 1024 * 1024
        ),
        name="middle",
    )(feat, weight, target, row_weight)


def plain_middle(features, weight, target, row_weight, scale, cells):
    response = jnp.einsum(
        "eokjc,kcd->eojd", features, weight, preferred_element_type=jnp.float32
    ).astype(jnp.bfloat16)
    member_total = features.shape[0] * lax.axis_size("ens")
    ensemble = lax.all_gather(response, "ens", axis=0, tiled=True)
    truth = target.astype(jnp.float32)[None]
    weighted, slopes = crps_terms(
        response.astype(jnp.float32), ensemble, truth, row_weight[None, :, None, None], member_total
    )
    loss_part = weighted / cells
    weight_part = jnp.einsum(
        "eokjc,eojd->kcd", features, slopes, preferred_element_type=jnp.float32
    )
    weight_sum, loss = lax.psum((weight_part, loss_part), ("lat", "lon", "ens"))
    feature_grad = jnp.einsum(
        "eojd,kcd->eokjc", slopes, weight, preferred_element_type=jnp.float32
    ).astype(jnp.bfloat16)
    return response, feature_grad, weight_sum * scale, loss


def per_device(inputs, weight, spread, target):
    ens_local, row_count, lon_count, channels = inputs.shape
    reach = HMAX
    lat_total = row_count * lax.axis_size("lat")
    lon_total = lon_count * lax.axis_size("lon")
    lon_first = lax.axis_index("lon") * lon_count
    global_rows = lax.axis_index("lat") * row_count + jnp.arange(row_count)
    polar_rows = (global_rows < PCAP) | (global_rows >= lat_total - PCAP)
    polar_mask = polar_rows[None, :, None, None, None]
    kernels = kernel_rows(spread, lon_count, reach)
    local_basis = circle_basis(lon_first, lon_count, lon_total)
    extended = extended_2(inputs, (("lat", 1),), 1, False)
    window = extended_2(extended, (("lon", 2),), reach, True)
    local_sums = jnp.einsum(
        "pj,erjc->eprc", local_basis, extended.astype(jnp.float32), precision=highest
    )
    circle_sums = lax.psum(local_sums, "lon")
    banded = jnp.concatenate(
        [
            jnp.einsum(
                "objq,eoqc->eobjc",
                kernels,
                window[:, lat_tap : lat_tap + row_count],
                preferred_element_type=jnp.float32,
            )
            for lat_tap in range(3)
        ],
        2,
    )
    rounds = circular(circle_sums, local_basis, lon_total, row_count)
    features = jnp.where(polar_mask, rounds, banded).astype(jnp.bfloat16)
    lat_weight = jnp.sin(math.pi * (global_rows.astype(jnp.float32) + 0.5) / lat_total)
    scale = math.sqrt(weight.shape[0] * channels) / (lat_total * lon_total)
    if ens_local == 1 and fits(row_count, lon_count, channels, weight.shape[0]):
        wide = jnp.broadcast_to(lat_weight[:, None, None], (row_count, 1, channels))
        response, feature_grad, grad_weight, loss_parts = run_middle(
            scale, features[0], weight, target, wide
        )
        response, feature_grad = response[None], feature_grad[None]
        loss = jnp.sum(loss_parts[:, 0]) / (lat_total * lon_total * channels)
    else:
        response, feature_grad, grad_weight, loss = plain_middle(
            features, weight, target, lat_weight, scale, lat_total * lon_total * channels
        )
    zero_grad = jnp.zeros_like(feature_grad)
    band_grad = jnp.where(polar_mask, zero_grad, feature_grad)
    circle_grad = jnp.where(polar_mask, feature_grad, zero_grad)
    window_grad = jnp.zeros(
        (ens_local, row_count + 2, lon_count + 2 * reach, channels), jnp.float32
    )
    sum_grad = jnp.zeros((ens_local, 3, row_count + 2, channels), jnp.float32)
    cos_wave = local_basis[1]
    sin_wave = local_basis[2]
    for lat_tap in range(3):
        picked = band_grad[:, :, 3 * lat_tap : 3 * lat_tap + 3]
        window_grad = window_grad.at[:, lat_tap : lat_tap + row_count].add(
            jnp.einsum("objq,eobjc->eoqc", kernels, picked, preferred_element_type=jnp.float32)
        )
        tap_grad = circle_grad[:, :, 3 * lat_tap : 3 * lat_tap + 3].astype(jnp.float32)
        mean_grad = jnp.sum(tap_grad[:, :, 0], axis=2) / lon_total
        cos_grad = (
            2.0
            / lon_total
            * (
                jnp.einsum("j,eojc->eoc", cos_wave, tap_grad[:, :, 1], precision=highest)
                - jnp.einsum("j,eojc->eoc", sin_wave, tap_grad[:, :, 2], precision=highest)
            )
        )
        sin_grad = (
            2.0
            / lon_total
            * (
                jnp.einsum("j,eojc->eoc", sin_wave, tap_grad[:, :, 1], precision=highest)
                + jnp.einsum("j,eojc->eoc", cos_wave, tap_grad[:, :, 2], precision=highest)
            )
        )
        sum_grad = sum_grad.at[:, :, lat_tap : lat_tap + row_count].add(
            jnp.stack([mean_grad, cos_grad, sin_grad], 1)
        )
    sum_total = lax.psum(sum_grad, "lon")
    core = window_grad[:, :, reach : reach + lon_count] + jnp.einsum(
        "pj,eprc->erjc", local_basis, sum_total, precision=highest
    )
    rims = jnp.concatenate([window_grad[:, :, :reach], window_grad[:, :, reach + lon_count :]], 2)
    arrived = extended_2(rims.astype(jnp.bfloat16), (("lon", 2),), reach, True).astype(rims.dtype)
    core = core.at[:, :, :reach].add(arrived[:, :, :reach])
    core = core.at[:, :, lon_count - reach :].add(arrived[:, :, 3 * reach :])
    edges = jnp.concatenate([core[:, :1], core[:, row_count + 1 :]], 1)
    arrived_rows = extended_2(edges.astype(jnp.bfloat16), (("lat", 1),), 1, False).astype(
        edges.dtype
    )
    inner = core[:, 1 : row_count + 1]
    inner = inner.at[:, 0].add(arrived_rows[:, 0])
    inner = inner.at[:, row_count - 1].add(arrived_rows[:, 3])
    return (response, inner.astype(jnp.bfloat16), grad_weight, loss)


def solution(mesh):
    in_specs = (P("ens", "lat", "lon", None), P(), P("lat"), P("lat", "lon", None))
    out_specs = (P("ens", "lat", "lon", None), P("ens", "lat", "lon", None), P(), P())
    return jax.shard_map(
        per_device, mesh=mesh, in_specs=in_specs, out_specs=out_specs, check_vma=False
    )
```

```python
import functools
import math

import jax
import jax.numpy as jnp
from jax import lax
from jax.experimental import pallas as pl
from jax.experimental.pallas import tpu as pltpu
from jax.sharding import PartitionSpec as P

PCAP = 2
HMAX = 16


highest = lax.Precision.HIGHEST


def extended_2(block, sides, width, periodic):
    for axis, dim in sides:
        count = lax.axis_size(axis)
        forward = [(i, i + 1) for i in range(count - 1)]
        if periodic:
            forward.append((count - 1, 0))
        backward = [(target, source) for source, target in forward]
        low = lax.ppermute(
            lax.slice_in_dim(block, block.shape[dim] - width, None, axis=dim), axis, forward
        )
        high = lax.ppermute(lax.slice_in_dim(block, 0, width, axis=dim), axis, backward)
        block = jnp.concatenate([low, block, high], axis=dim)
    return block


def kernel_rows(spread_rows, lon_count, reach):
    halves = spread_rows.astype(jnp.float32)[:, None, None, None] / 2.0
    columns = jnp.arange(lon_count)
    window_cols = jnp.arange(lon_count + 2 * reach)
    offsets = (window_cols[None, :] - reach - columns[:, None]).astype(jnp.float32)
    centres = (jnp.arange(3) - 1).astype(jnp.float32)[None, :, None, None] * halves
    values = jnp.maximum(0.0, 1.0 - jnp.abs(offsets[None, None] - centres) / halves) / halves
    return values.astype(jnp.bfloat16)


def circle_basis(first_col, lon_count, circle):
    angles = 2.0 * math.pi * (first_col + jnp.arange(lon_count)).astype(jnp.float32) / circle
    return jnp.stack([jnp.ones_like(angles), jnp.cos(angles), jnp.sin(angles)])


def circular(circle_sums, basis, circle, row_count):
    cos_wave = basis[1][None, None, :, None]
    sin_wave = basis[2][None, None, :, None]
    pieces = []
    for lat_tap in range(3):
        tap_sums = circle_sums[:, :, lat_tap : lat_tap + row_count]
        mean_part = tap_sums[:, 0][:, :, None, :] / circle
        cosine_part = (
            2.0
            / circle
            * (cos_wave * tap_sums[:, 1][:, :, None, :] + sin_wave * tap_sums[:, 2][:, :, None, :])
        )
        sine_part = (
            2.0
            / circle
            * (cos_wave * tap_sums[:, 2][:, :, None, :] - sin_wave * tap_sums[:, 1][:, :, None, :])
        )
        pieces += [jnp.broadcast_to(mean_part, cosine_part.shape), cosine_part, sine_part]
    return jnp.stack(pieces, 2)


def crps_terms(values, every_member, truth, lat_weight, member_total):
    miss = values - truth
    own_dist = jnp.sqrt(miss * miss + 0.25)
    own_slope = miss / own_dist

    def add_member(member, carry):
        pair_dist, pair_slope = carry
        other = lax.dynamic_index_in_dim(every_member, member, 0, keepdims=True).astype(jnp.float32)
        gap_value = values - other
        distance = jnp.sqrt(gap_value * gap_value + 0.25)
        return (pair_dist + distance, pair_slope + gap_value / distance)

    start = (jnp.zeros_like(values), jnp.zeros_like(values))
    pair_dist, pair_slope = lax.fori_loop(0, member_total, add_member, start)
    pair_dist = pair_dist - 0.5
    scores = own_dist / member_total - pair_dist / (2 * member_total * (member_total - 1))
    weighted = jnp.sum(lat_weight * scores)
    slopes = (
        lat_weight * (own_slope / member_total - pair_slope / (member_total * (member_total - 1)))
    ).astype(jnp.bfloat16)
    return (weighted, slopes)


MESH = pl.DeviceIdType.MESH
ROWDOT = (((0,), (0,)), ((), ()))
COLDOT = (((1,), (1,)), ((), ()))


def pick_tile(lon_count):
    for tile in (240, 144, 96, 80, 48, 32, 16):
        if lon_count % tile == 0:
            return tile
    return 0


def fits(row_count, lon_count, channels, taps):
    lats, lons, members = (lax.axis_size(a) for a in ("lat", "lon", "ens"))
    return (
        lons == 2
        and members <= 8
        and lats <= 8
        and channels % 256 == 0
        and pick_tile(lon_count) > 0
        and (taps * channels) % (16 * lats * members) == 0
    )


def middle(scale, feat, weight, target, row_weight, resp, fg, grad_w, loss, rsp, gath, acc, losses,
           send1, recv1, out2, in2, red2, out3, in3, red3, full, sems, loss_sems):
    members, lats = lax.axis_size("ens"), lax.axis_size("lat")
    me, my_lat, my_lon = lax.axis_index("ens"), lax.axis_index("lat"), lax.axis_index("lon")
    rows, taps, lon_count, channels = feat.shape
    tile = pick_tile(lon_count)
    per_row = lon_count // tile
    chunks = rows * per_row
    half = channels // 2

    def peer(axis, here, count, step):
        return {axis: lax.rem(here + step, count)}

    barrier = pltpu.get_barrier_semaphore()
    peers = (
        [peer("ens", me, members, p) for p in range(1, members)]
        + [peer("lat", my_lat, lats, p) for p in range(1, lats)]
        + [{"lon": 1 - my_lon}]
    )
    for other in peers:
        pl.semaphore_signal(barrier, inc=1, device_id=other, device_id_type=MESH)
    pl.semaphore_wait(barrier, len(peers))

    def where(i):
        return i // per_row, pl.ds(pl.multiple_of(lax.rem(i, per_row) * tile, 16), tile)

    def gather_copy(i, p):
        o, cols = where(i)
        return pltpu.make_async_remote_copy(
            src_ref=rsp.at[o, cols], dst_ref=gath.at[p - 1, o, cols],
            send_sem=send1.at[p - 1, i], recv_sem=recv1.at[p - 1, i],
            device_id=peer("ens", me, members, p), device_id_type=MESH,
        )

    def forward(i, carry):
        o, cols = where(i)
        total = jnp.zeros((tile, channels), jnp.float32)
        for k in range(taps):
            total = total + jnp.dot(feat[o, k, cols], weight[k], preferred_element_type=jnp.float32)
        rsp[o, cols] = total.astype(jnp.bfloat16)
        for p in range(1, members):
            gather_copy(i, p).start()
        return carry

    lax.fori_loop(0, chunks, forward, 0)
    resp[...] = rsp[...]
    acc[...] = jnp.zeros_like(acc)

    def backward(i, carry):
        o, cols = where(i)
        for p in range(1, members):
            gather_copy(i, p).wait_recv()
        value = rsp[o, cols].astype(jnp.float32)
        miss = value - target[o, cols].astype(jnp.float32)
        square = miss * miss + 0.25
        inverse = lax.rsqrt(square)
        own_dist = square * inverse
        own_slope = miss * inverse
        pair_dist = jnp.zeros_like(value)
        pair_slope = jnp.zeros_like(value)
        for p in range(1, members):
            gap = value - gath[p - 1, o, cols].astype(jnp.float32)
            square = gap * gap + 0.25
            inverse = lax.rsqrt(square)
            pair_dist = pair_dist + square * inverse
            pair_slope = pair_slope + gap * inverse
        lat_weight = row_weight[o]
        score = own_dist / members - pair_dist / (2 * members * (members - 1))
        slope = lat_weight * (own_slope / members - pair_slope / (members * (members - 1)))
        slope = slope.astype(jnp.bfloat16)
        score = lat_weight * jnp.sum(score.reshape(tile // 8, 8, channels), axis=0)
        for k in range(taps):
            part = lax.dot_general(feat[o, k, cols], slope, ROWDOT, preferred_element_type=jnp.float32)
            for h in range(2):
                acc[h, pl.ds(k * channels, channels)] += part[:, h * half : (h + 1) * half]
            fg[o, k, cols] = lax.dot_general(
                slope, weight[k], COLDOT, preferred_element_type=jnp.float32
            ).astype(jnp.bfloat16)
        return carry + score

    score = lax.fori_loop(0, chunks, backward, jnp.zeros((8, channels), jnp.float32))
    part_loss = jnp.sum(score, axis=1, keepdims=True) * jnp.ones((8, 128), jnp.float32)

    def remote(src, dst, at, other):
        return pltpu.make_async_remote_copy(
            src_ref=src, dst_ref=dst, send_sem=sems.at[0, at], recv_sem=sems.at[1, at],
            device_id=other, device_id_type=MESH,
        )

    def remote_loss(src, dst, at, other):
        return pltpu.make_async_remote_copy(
            src_ref=src, dst_ref=dst, send_sem=loss_sems.at[0, at], recv_sem=loss_sems.at[1, at],
            device_id=other, device_id_type=MESH,
        )

    def finish(copies):
        for copy in copies:
            copy.wait_recv()

    pending = []
    at, lat_at = 0, 0
    out2[...] = acc[1 - my_lon].astype(jnp.bfloat16).reshape(out2.shape)
    losses[0] = part_loss
    copies = [
        remote(out2, in2, at, {"lon": 1 - my_lon}),
        remote_loss(losses.at[0], losses.at[1], lat_at, {"lon": 1 - my_lon}),
    ]
    for copy in copies:
        copy.start()
    finish(copies)
    pending += copies
    at, lat_at = at + 1, lat_at + 1
    red2[...] = acc[my_lon].reshape(red2.shape) + in2[...].astype(jnp.float32)
    base = 2
    losses[base + my_lat] = losses[0] + losses[1]
    send2 = out3
    send2[...] = red2[...].astype(jnp.bfloat16)
    copies = []
    for p in range(1, lats):
        other = peer("lat", my_lat, lats, p)
        copies.append(remote(send2.at[other["lat"]], in3.at[p - 1], at, other))
        copies.append(remote_loss(losses.at[base + my_lat], losses.at[base + my_lat], lat_at, other))
        at, lat_at = at + 1, lat_at + 1
    for copy in copies:
        copy.start()
    finish(copies)
    pending += copies
    total = red2[my_lat]
    for p in range(1, lats):
        total = total + in3[p - 1].astype(jnp.float32)
    parts = red3.shape[0]
    red3[...] = total.reshape(parts, total.shape[0] // parts, half)
    total = losses[base]
    for p in range(1, lats):
        total = total + losses[base + p]
    base = base + lats
    losses[base + me] = total
    red_out, red_in = full_split(full, members)
    red_out[...] = red3[...].astype(jnp.bfloat16)
    copies = []
    for p in range(1, members):
        other = peer("ens", me, members, p)
        copies.append(remote(red_out.at[other["ens"]], red_in.at[p - 1], at, other))
        copies.append(remote_loss(losses.at[base + me], losses.at[base + me], lat_at, other))
        at, lat_at = at + 1, lat_at + 1
    for copy in copies:
        copy.start()
    finish(copies)
    pending += copies
    total = red3[me]
    for p in range(1, members):
        total = total + red_in[p - 1].astype(jnp.float32)
    gathered = full[2]
    gathered[my_lon, my_lat, me] = (total * scale).astype(jnp.bfloat16)
    total = losses[base]
    for p in range(1, members):
        total = total + losses[base + p]
    loss[...] = total
    mine = gathered.at[my_lon, my_lat, me]
    copies = []
    for p in range(1, members):
        copies.append(remote(mine, mine, at, peer("ens", me, members, p)))
        at += 1
    for copy in copies:
        copy.start()
    finish(copies)
    pending += copies
    mine = gathered.at[my_lon, my_lat]
    copies = []
    for p in range(1, lats):
        copies.append(remote(mine, mine, at, peer("lat", my_lat, lats, p)))
        at += 1
    for copy in copies:
        copy.start()
    finish(copies)
    pending += copies
    mine = gathered.at[my_lon]
    copies = [remote(mine, mine, at, {"lon": 1 - my_lon})]
    copies[0].start()
    finish(copies)
    pending += copies
    for h in range(2):
        grad_w[:, :, h * half : (h + 1) * half] = (
            gathered[h].astype(jnp.float32).reshape(taps, channels, half)
        )
    for copy in pending:
        copy.wait_send()

    def drain(i, carry):
        for p in range(1, members):
            gather_copy(i, p).wait_send()
        return carry

    lax.fori_loop(0, chunks, drain, 0)


def full_split(full, members):
    return full[0], full[1]


def run_middle(scale, feat, weight, target, row_weight):
    members, lats = lax.axis_size("ens"), lax.axis_size("lat")
    rows, taps, lon_count, channels = feat.shape
    chunks = rows * (lon_count // pick_tile(lon_count))
    half = channels // 2
    flat = taps * channels
    band, piece = flat // lats, flat // lats // members
    bf16, f32 = jnp.bfloat16, jnp.float32
    shape = jax.ShapeDtypeStruct
    whole = pl.BlockSpec(memory_space=pltpu.VMEM)
    count = 1 + 2 * (lats - 1) + 2 * (members - 1) + 1
    loss_count = 1 + (lats - 1) + (members - 1)
    return pl.pallas_call(
        functools.partial(middle, scale),
        out_shape=[
            shape((rows, lon_count, channels), bf16),
            shape(feat.shape, bf16),
            shape((taps, channels, channels), f32),
            shape((8, 128), f32),
        ],
        in_specs=[whole] * 4,
        out_specs=[whole] * 4,
        scratch_shapes=[
            pltpu.VMEM((rows, lon_count, channels), bf16),
            pltpu.VMEM((members - 1, rows, lon_count, channels), bf16),
            pltpu.VMEM((2, flat, half), f32),
            pltpu.VMEM((2 + lats + members, 8, 128), f32),
            pltpu.SemaphoreType.DMA((members - 1, chunks)),
            pltpu.SemaphoreType.DMA((members - 1, chunks)),
            pltpu.VMEM((lats, band, half), bf16),
            pltpu.VMEM((lats, band, half), bf16),
            pltpu.VMEM((lats, band, half), f32),
            pltpu.VMEM((lats, band, half), bf16),
            pltpu.VMEM((lats - 1, band, half), bf16),
            pltpu.VMEM((members, piece, half), f32),
            [
                pltpu.VMEM((members, piece, half), bf16),
                pltpu.VMEM((members - 1, piece, half), bf16),
                pltpu.VMEM((2, lats, members, piece, half), bf16),
            ],
            pltpu.SemaphoreType.DMA((2, count)),
            pltpu.SemaphoreType.DMA((2, loss_count)),
        ],
        compiler_params=pltpu.CompilerParams(
            collective_id=0, has_side_effects=True, vmem_limit_bytes=50 * 1024 * 1024
        ),
        name="middle",
    )(feat, weight, target, row_weight)


def plain_middle(features, weight, target, row_weight, scale, cells):
    response = jnp.einsum(
        "eokjc,kcd->eojd", features, weight, preferred_element_type=jnp.float32
    ).astype(jnp.bfloat16)
    member_total = features.shape[0] * lax.axis_size("ens")
    ensemble = lax.all_gather(response, "ens", axis=0, tiled=True)
    truth = target.astype(jnp.float32)[None]
    weighted, slopes = crps_terms(
        response.astype(jnp.float32), ensemble, truth, row_weight[None, :, None, None], member_total
    )
    loss_part = weighted / cells
    weight_part = jnp.einsum(
        "eokjc,eojd->kcd", features, slopes, preferred_element_type=jnp.float32
    )
    weight_sum, loss = lax.psum((weight_part, loss_part), ("lat", "lon", "ens"))
    feature_grad = jnp.einsum(
        "eojd,kcd->eokjc", slopes, weight, preferred_element_type=jnp.float32
    ).astype(jnp.bfloat16)
    return response, feature_grad, weight_sum * scale, loss


def lon_sum(value):
    if lax.axis_size("lon") == 2:
        return value + lax.ppermute(value, "lon", [(0, 1), (1, 0)])
    return lax.psum(value, "lon")


def lat_swap(down, up):
    count = lax.axis_size("lat")
    forward = [(i, i + 1) for i in range(count - 1)]
    backward = [(target, source) for source, target in forward]
    return lax.ppermute(down, "lat", backward), lax.ppermute(up, "lat", forward)


def per_device(inputs, weight, spread, target):
    ens_local, row_count, lon_count, channels = inputs.shape
    reach = HMAX
    lat_total = row_count * lax.axis_size("lat")
    lon_total = lon_count * lax.axis_size("lon")
    lon_first = lax.axis_index("lon") * lon_count
    global_rows = lax.axis_index("lat") * row_count + jnp.arange(row_count)
    polar_rows = (global_rows < PCAP) | (global_rows >= lat_total - PCAP)
    polar_mask = polar_rows[None, :, None, None, None]
    kernels = kernel_rows(spread, lon_count, reach)
    local_basis = circle_basis(lon_first, lon_count, lon_total)
    extended = extended_2(inputs, (("lat", 1),), 1, False)
    local_sums = jnp.einsum(
        "pj,erjc->eprc", local_basis, extended.astype(jnp.float32), precision=highest
    )
    circle_sums = lon_sum(local_sums)
    own = extended_2(inputs, (("lon", 2),), reach, True)
    edge_rows = jnp.concatenate([extended[:, :1], extended[:, row_count + 1 :]], 1)
    beyond = extended_2(edge_rows, (("lon", 2),), reach, True)

    def banded_row(row, lat_tap):
        source = row + lat_tap - 1
        if source < 0:
            strip = beyond[:, 0]
        elif source >= row_count:
            strip = beyond[:, 1]
        else:
            strip = own[:, source]
        return jnp.einsum(
            "bjq,eqc->ebjc", kernels[row], strip, preferred_element_type=jnp.float32
        )

    banded = jnp.stack(
        [
            jnp.concatenate([banded_row(row, lat_tap) for lat_tap in range(3)], 1)
            for row in range(row_count)
        ],
        1,
    )
    rounds = circular(circle_sums, local_basis, lon_total, row_count)
    features = jnp.where(polar_mask, rounds, banded).astype(jnp.bfloat16)
    lat_weight = jnp.sin(math.pi * (global_rows.astype(jnp.float32) + 0.5) / lat_total)
    scale = math.sqrt(weight.shape[0] * channels) / (lat_total * lon_total)
    if ens_local == 1 and fits(row_count, lon_count, channels, weight.shape[0]):
        wide = jnp.broadcast_to(lat_weight[:, None, None], (row_count, 1, channels))
        response, feature_grad, grad_weight, loss_parts = run_middle(
            scale, features[0], weight, target, wide
        )
        response, feature_grad = response[None], feature_grad[None]
        loss = jnp.sum(loss_parts[:, 0]) / (lat_total * lon_total * channels)
    else:
        response, feature_grad, grad_weight, loss = plain_middle(
            features, weight, target, lat_weight, scale, lat_total * lon_total * channels
        )
    band_kernels = jnp.where(polar_rows[:, None, None, None], 0.0, kernels).astype(jnp.bfloat16)
    high = local_basis.astype(jnp.bfloat16)
    low = (local_basis - high.astype(jnp.float32)).astype(jnp.bfloat16)
    waves = jnp.einsum(
        "pj,eokjc->eokpc",
        jnp.concatenate([high, low]),
        feature_grad,
        preferred_element_type=jnp.float32,
    )
    waves = waves[:, :, :, :3] + waves[:, :, :, 3:]
    waves = jnp.where(polar_mask, waves, 0.0)

    def circle_row(row, lat_tap):
        taps = waves[:, row, 3 * lat_tap : 3 * lat_tap + 3]
        mean_grad = taps[:, 0, 0] / lon_total
        cos_grad = 2.0 / lon_total * (taps[:, 1, 1] - taps[:, 2, 2])
        sin_grad = 2.0 / lon_total * (taps[:, 1, 2] + taps[:, 2, 1])
        return jnp.stack([mean_grad, cos_grad, sin_grad], 1)

    def band_row(row, lat_tap):
        return jnp.einsum(
            "bjq,ebjc->eqc",
            band_kernels[row],
            feature_grad[:, row, 3 * lat_tap : 3 * lat_tap + 3],
            preferred_element_type=jnp.float32,
        )

    last = row_count - 1
    down_window, up_window = lat_swap(
        band_row(0, 0).astype(jnp.bfloat16), band_row(last, 2).astype(jnp.bfloat16)
    )
    down_sums, up_sums = lat_swap(circle_row(0, 0), circle_row(last, 2))
    sum_rows, window_rows = [], []
    for source in range(row_count):
        pairs = [(row, source - row + 1) for row in range(row_count) if 0 <= source - row + 1 <= 2]
        sums = sum(circle_row(*pair) for pair in pairs)
        window = sum(band_row(*pair) for pair in pairs)
        if source == 0:
            sums, window = sums + up_sums, window + up_window.astype(jnp.float32)
        if source == last:
            sums, window = sums + down_sums, window + down_window.astype(jnp.float32)
        sum_rows.append(sums)
        window_rows.append(window)
    sum_total = lon_sum(jnp.stack(sum_rows, 2))
    window_grad = jnp.stack(window_rows, 1)
    circle_part = sum(
        local_basis[p][None, None, :, None] * sum_total[:, p][:, :, None, :] for p in range(3)
    )
    core = window_grad[:, :, reach : reach + lon_count] + circle_part
    rims = jnp.concatenate([window_grad[:, :, :reach], window_grad[:, :, reach + lon_count :]], 2)
    arrived = extended_2(rims.astype(jnp.bfloat16), (("lon", 2),), reach, True).astype(rims.dtype)
    core = jnp.concatenate(
        [
            core[:, :, :reach] + arrived[:, :, :reach],
            core[:, :, reach : lon_count - reach],
            core[:, :, lon_count - reach :] + arrived[:, :, 3 * reach :],
        ],
        2,
    )
    return (response, core.astype(jnp.bfloat16), grad_weight, loss)


def solution(mesh):
    in_specs = (P("ens", "lat", "lon", None), P(), P("lat"), P("lat", "lon", None))
    out_specs = (P("ens", "lat", "lon", None), P("ens", "lat", "lon", None), P(), P())
    return jax.shard_map(
        per_device, mesh=mesh, in_specs=in_specs, out_specs=out_specs, check_vma=False
    )
```

```python
import functools
import math

import jax
import jax.numpy as jnp
from jax import lax
from jax.experimental import pallas as pl
from jax.experimental.pallas import tpu as pltpu
from jax.sharding import PartitionSpec as P

PCAP = 2
HMAX = 16


highest = lax.Precision.HIGHEST


def extended_2(block, sides, width, periodic):
    for axis, dim in sides:
        count = lax.axis_size(axis)
        forward = [(i, i + 1) for i in range(count - 1)]
        if periodic:
            forward.append((count - 1, 0))
        backward = [(target, source) for source, target in forward]
        low = lax.ppermute(
            lax.slice_in_dim(block, block.shape[dim] - width, None, axis=dim), axis, forward
        )
        high = lax.ppermute(lax.slice_in_dim(block, 0, width, axis=dim), axis, backward)
        block = jnp.concatenate([low, block, high], axis=dim)
    return block


def kernel_rows(spread_rows, lon_count, reach):
    halves = spread_rows.astype(jnp.float32)[:, None, None, None] / 2.0
    columns = jnp.arange(lon_count)
    window_cols = jnp.arange(lon_count + 2 * reach)
    offsets = (window_cols[None, :] - reach - columns[:, None]).astype(jnp.float32)
    centres = (jnp.arange(3) - 1).astype(jnp.float32)[None, :, None, None] * halves
    values = jnp.maximum(0.0, 1.0 - jnp.abs(offsets[None, None] - centres) / halves) / halves
    return values.astype(jnp.bfloat16)


def circle_basis(first_col, lon_count, circle):
    angles = 2.0 * math.pi * (first_col + jnp.arange(lon_count)).astype(jnp.float32) / circle
    return jnp.stack([jnp.ones_like(angles), jnp.cos(angles), jnp.sin(angles)])


def circular(circle_sums, basis, circle, row_count):
    cos_wave = basis[1][None, None, :, None]
    sin_wave = basis[2][None, None, :, None]
    pieces = []
    for lat_tap in range(3):
        tap_sums = circle_sums[:, :, lat_tap : lat_tap + row_count]
        mean_part = tap_sums[:, 0][:, :, None, :] / circle
        cosine_part = (
            2.0
            / circle
            * (cos_wave * tap_sums[:, 1][:, :, None, :] + sin_wave * tap_sums[:, 2][:, :, None, :])
        )
        sine_part = (
            2.0
            / circle
            * (cos_wave * tap_sums[:, 2][:, :, None, :] - sin_wave * tap_sums[:, 1][:, :, None, :])
        )
        pieces += [jnp.broadcast_to(mean_part, cosine_part.shape), cosine_part, sine_part]
    return jnp.stack(pieces, 2)


def crps_terms(values, every_member, truth, lat_weight, member_total):
    miss = values - truth
    own_dist = jnp.sqrt(miss * miss + 0.25)
    own_slope = miss / own_dist

    def add_member(member, carry):
        pair_dist, pair_slope = carry
        other = lax.dynamic_index_in_dim(every_member, member, 0, keepdims=True).astype(jnp.float32)
        gap_value = values - other
        distance = jnp.sqrt(gap_value * gap_value + 0.25)
        return (pair_dist + distance, pair_slope + gap_value / distance)

    start = (jnp.zeros_like(values), jnp.zeros_like(values))
    pair_dist, pair_slope = lax.fori_loop(0, member_total, add_member, start)
    pair_dist = pair_dist - 0.5
    scores = own_dist / member_total - pair_dist / (2 * member_total * (member_total - 1))
    weighted = jnp.sum(lat_weight * scores)
    slopes = (
        lat_weight * (own_slope / member_total - pair_slope / (member_total * (member_total - 1)))
    ).astype(jnp.bfloat16)
    return (weighted, slopes)


MESH = pl.DeviceIdType.MESH
ROWDOT = (((0,), (0,)), ((), ()))
COLDOT = (((1,), (1,)), ((), ()))


def pick_tile(lon_count):
    for tile in (240, 144, 96, 80, 48, 32, 16):
        if lon_count % tile == 0:
            return tile
    return 0


def fits(row_count, lon_count, channels, taps):
    lats, lons, members = (lax.axis_size(a) for a in ("lat", "lon", "ens"))
    return (
        lons == 2
        and members <= 8
        and lats <= 8
        and channels % 256 == 0
        and pick_tile(lon_count) > 0
        and (taps * channels) % (16 * lats * members) == 0
    )


def middle(scale, feat, weight, target, row_weight, resp, fg, grad_w, loss, rsp, gath, acc, losses,
           send1, recv1, slopes, out2, in2, red2, out3, in3, red3, full, sems, loss_sems):
    members, lats = lax.axis_size("ens"), lax.axis_size("lat")
    me, my_lat, my_lon = lax.axis_index("ens"), lax.axis_index("lat"), lax.axis_index("lon")
    rows, taps, lon_count, channels = feat.shape
    tile = pick_tile(lon_count)
    per_row = lon_count // tile
    chunks = rows * per_row
    half = channels // 2

    def peer(axis, here, count, step):
        return {axis: lax.rem(here + step, count)}

    barrier = pltpu.get_barrier_semaphore()
    peers = (
        [peer("ens", me, members, p) for p in range(1, members)]
        + [peer("lat", my_lat, lats, p) for p in range(1, lats)]
        + [{"lon": 1 - my_lon}]
    )
    for other in peers:
        pl.semaphore_signal(barrier, inc=1, device_id=other, device_id_type=MESH)
    pl.semaphore_wait(barrier, len(peers))

    def where(i):
        return i // per_row, pl.ds(pl.multiple_of(lax.rem(i, per_row) * tile, 16), tile)

    def gather_copy(i, p):
        o, cols = where(i)
        return pltpu.make_async_remote_copy(
            src_ref=rsp.at[o, cols], dst_ref=gath.at[p - 1, o, cols],
            send_sem=send1.at[p - 1, i], recv_sem=recv1.at[p - 1, i],
            device_id=peer("ens", me, members, p), device_id_type=MESH,
        )

    def forward(i, carry):
        o, cols = where(i)
        total = jnp.zeros((tile, channels), jnp.float32)
        for k in range(taps):
            total = total + jnp.dot(feat[o, k, cols], weight[k], preferred_element_type=jnp.float32)
        rsp[o, cols] = total.astype(jnp.bfloat16)
        for p in range(1, members):
            gather_copy(i, p).start()
        return carry

    lax.fori_loop(0, chunks, forward, 0)
    resp[...] = rsp[...]
    acc[...] = jnp.zeros_like(acc)

    def backward(i, carry):
        o, cols = where(i)
        for p in range(1, members):
            gather_copy(i, p).wait_recv()
        value = rsp[o, cols].astype(jnp.float32)
        miss = value - target[o, cols].astype(jnp.float32)
        square = miss * miss + 0.25
        inverse = lax.rsqrt(square)
        own_dist = square * inverse
        own_slope = miss * inverse
        pair_dist = jnp.zeros_like(value)
        pair_slope = jnp.zeros_like(value)
        for p in range(1, members):
            gap = value - gath[p - 1, o, cols].astype(jnp.float32)
            square = gap * gap + 0.25
            inverse = lax.rsqrt(square)
            pair_dist = pair_dist + square * inverse
            pair_slope = pair_slope + gap * inverse
        lat_weight = row_weight[o]
        score = own_dist / members - pair_dist / (2 * members * (members - 1))
        slope = lat_weight * (own_slope / members - pair_slope / (members * (members - 1)))
        slope = slope.astype(jnp.bfloat16)
        score = lat_weight * jnp.sum(score.reshape(tile // 8, 8, channels), axis=0)
        for k in range(taps):
            part = lax.dot_general(feat[o, k, cols], slope, ROWDOT, preferred_element_type=jnp.float32)
            for h in range(2):
                acc[h, pl.ds(k * channels, channels)] += part[:, h * half : (h + 1) * half]
        slopes[o, cols] = slope
        return carry + score

    stages = 6

    def beside(stage):
        def spread_back(i, carry):
            o, cols = where(i)
            for k in range(taps):
                fg[o, k, cols] = lax.dot_general(
                    slopes[o, cols], weight[k], COLDOT, preferred_element_type=jnp.float32
                ).astype(jnp.bfloat16)
            return carry

        lax.fori_loop(chunks * stage // stages, chunks * (stage + 1) // stages, spread_back, 0)

    score = lax.fori_loop(0, chunks, backward, jnp.zeros((8, channels), jnp.float32))
    part_loss = jnp.sum(score, axis=1, keepdims=True) * jnp.ones((8, 128), jnp.float32)

    def remote(src, dst, at, other):
        return pltpu.make_async_remote_copy(
            src_ref=src, dst_ref=dst, send_sem=sems.at[0, at], recv_sem=sems.at[1, at],
            device_id=other, device_id_type=MESH,
        )

    def remote_loss(src, dst, at, other):
        return pltpu.make_async_remote_copy(
            src_ref=src, dst_ref=dst, send_sem=loss_sems.at[0, at], recv_sem=loss_sems.at[1, at],
            device_id=other, device_id_type=MESH,
        )

    def finish(copies):
        for copy in copies:
            copy.wait_recv()

    pending = []
    at, lat_at = 0, 0
    out2[...] = acc[1 - my_lon].astype(jnp.bfloat16).reshape(out2.shape)
    losses[0] = part_loss
    copies = [
        remote(out2, in2, at, {"lon": 1 - my_lon}),
        remote_loss(losses.at[0], losses.at[1], lat_at, {"lon": 1 - my_lon}),
    ]
    for copy in copies:
        copy.start()
    beside(0)
    finish(copies)
    pending += copies
    at, lat_at = at + 1, lat_at + 1
    red2[...] = acc[my_lon].reshape(red2.shape) + in2[...].astype(jnp.float32)
    base = 2
    losses[base + my_lat] = losses[0] + losses[1]
    send2 = out3
    send2[...] = red2[...].astype(jnp.bfloat16)
    copies = []
    for p in range(1, lats):
        other = peer("lat", my_lat, lats, p)
        copies.append(remote(send2.at[other["lat"]], in3.at[p - 1], at, other))
        copies.append(remote_loss(losses.at[base + my_lat], losses.at[base + my_lat], lat_at, other))
        at, lat_at = at + 1, lat_at + 1
    for copy in copies:
        copy.start()
    beside(1)
    finish(copies)
    pending += copies
    total = red2[my_lat]
    for p in range(1, lats):
        total = total + in3[p - 1].astype(jnp.float32)
    parts = red3.shape[0]
    red3[...] = total.reshape(parts, total.shape[0] // parts, half)
    total = losses[base]
    for p in range(1, lats):
        total = total + losses[base + p]
    base = base + lats
    losses[base + me] = total
    red_out, red_in = full_split(full, members)
    red_out[...] = red3[...].astype(jnp.bfloat16)
    copies = []
    for p in range(1, members):
        other = peer("ens", me, members, p)
        copies.append(remote(red_out.at[other["ens"]], red_in.at[p - 1], at, other))
        copies.append(remote_loss(losses.at[base + me], losses.at[base + me], lat_at, other))
        at, lat_at = at + 1, lat_at + 1
    for copy in copies:
        copy.start()
    beside(2)
    finish(copies)
    pending += copies
    total = red3[me]
    for p in range(1, members):
        total = total + red_in[p - 1].astype(jnp.float32)
    gathered = full[2]
    gathered[my_lon, my_lat, me] = (total * scale).astype(jnp.bfloat16)
    total = losses[base]
    for p in range(1, members):
        total = total + losses[base + p]
    loss[...] = total
    mine = gathered.at[my_lon, my_lat, me]
    copies = []
    for p in range(1, members):
        copies.append(remote(mine, mine, at, peer("ens", me, members, p)))
        at += 1
    for copy in copies:
        copy.start()
    beside(3)
    finish(copies)
    pending += copies
    mine = gathered.at[my_lon, my_lat]
    copies = []
    for p in range(1, lats):
        copies.append(remote(mine, mine, at, peer("lat", my_lat, lats, p)))
        at += 1
    for copy in copies:
        copy.start()
    beside(4)
    finish(copies)
    pending += copies
    mine = gathered.at[my_lon]
    copies = [remote(mine, mine, at, {"lon": 1 - my_lon})]
    copies[0].start()
    beside(5)
    finish(copies)
    pending += copies
    for h in range(2):
        grad_w[:, :, h * half : (h + 1) * half] = (
            gathered[h].astype(jnp.float32).reshape(taps, channels, half)
        )
    for copy in pending:
        copy.wait_send()

    def drain(i, carry):
        for p in range(1, members):
            gather_copy(i, p).wait_send()
        return carry

    lax.fori_loop(0, chunks, drain, 0)


def full_split(full, members):
    return full[0], full[1]


def run_middle(scale, feat, weight, target, row_weight):
    members, lats = lax.axis_size("ens"), lax.axis_size("lat")
    rows, taps, lon_count, channels = feat.shape
    chunks = rows * (lon_count // pick_tile(lon_count))
    half = channels // 2
    flat = taps * channels
    band, piece = flat // lats, flat // lats // members
    bf16, f32 = jnp.bfloat16, jnp.float32
    shape = jax.ShapeDtypeStruct
    whole = pl.BlockSpec(memory_space=pltpu.VMEM)
    count = 1 + 2 * (lats - 1) + 2 * (members - 1) + 1
    loss_count = 1 + (lats - 1) + (members - 1)
    return pl.pallas_call(
        functools.partial(middle, scale),
        out_shape=[
            shape((rows, lon_count, channels), bf16),
            shape(feat.shape, bf16),
            shape((taps, channels, channels), f32),
            shape((8, 128), f32),
        ],
        in_specs=[whole] * 4,
        out_specs=[whole] * 4,
        scratch_shapes=[
            pltpu.VMEM((rows, lon_count, channels), bf16),
            pltpu.VMEM((members - 1, rows, lon_count, channels), bf16),
            pltpu.VMEM((2, flat, half), f32),
            pltpu.VMEM((2 + lats + members, 8, 128), f32),
            pltpu.SemaphoreType.DMA((members - 1, chunks)),
            pltpu.SemaphoreType.DMA((members - 1, chunks)),
            pltpu.VMEM((rows, lon_count, channels), bf16),
            pltpu.VMEM((lats, band, half), bf16),
            pltpu.VMEM((lats, band, half), bf16),
            pltpu.VMEM((lats, band, half), f32),
            pltpu.VMEM((lats, band, half), bf16),
            pltpu.VMEM((lats - 1, band, half), bf16),
            pltpu.VMEM((members, piece, half), f32),
            [
                pltpu.VMEM((members, piece, half), bf16),
                pltpu.VMEM((members - 1, piece, half), bf16),
                pltpu.VMEM((2, lats, members, piece, half), bf16),
            ],
            pltpu.SemaphoreType.DMA((2, count)),
            pltpu.SemaphoreType.DMA((2, loss_count)),
        ],
        compiler_params=pltpu.CompilerParams(
            collective_id=0, has_side_effects=True, vmem_limit_bytes=50 * 1024 * 1024
        ),
        name="middle",
    )(feat, weight, target, row_weight)


def plain_middle(features, weight, target, row_weight, scale, cells):
    response = jnp.einsum(
        "eokjc,kcd->eojd", features, weight, preferred_element_type=jnp.float32
    ).astype(jnp.bfloat16)
    member_total = features.shape[0] * lax.axis_size("ens")
    ensemble = lax.all_gather(response, "ens", axis=0, tiled=True)
    truth = target.astype(jnp.float32)[None]
    weighted, slopes = crps_terms(
        response.astype(jnp.float32), ensemble, truth, row_weight[None, :, None, None], member_total
    )
    loss_part = weighted / cells
    weight_part = jnp.einsum(
        "eokjc,eojd->kcd", features, slopes, preferred_element_type=jnp.float32
    )
    weight_sum, loss = lax.psum((weight_part, loss_part), ("lat", "lon", "ens"))
    feature_grad = jnp.einsum(
        "eojd,kcd->eokjc", slopes, weight, preferred_element_type=jnp.float32
    ).astype(jnp.bfloat16)
    return response, feature_grad, weight_sum * scale, loss


def lon_sum(value):
    if lax.axis_size("lon") == 2:
        return value + lax.ppermute(value, "lon", [(0, 1), (1, 0)])
    return lax.psum(value, "lon")


def lat_swap(down, up):
    count = lax.axis_size("lat")
    forward = [(i, i + 1) for i in range(count - 1)]
    backward = [(target, source) for source, target in forward]
    return lax.ppermute(down, "lat", backward), lax.ppermute(up, "lat", forward)


def per_device(inputs, weight, spread, target):
    ens_local, row_count, lon_count, channels = inputs.shape
    reach = HMAX
    lat_total = row_count * lax.axis_size("lat")
    lon_total = lon_count * lax.axis_size("lon")
    lon_first = lax.axis_index("lon") * lon_count
    global_rows = lax.axis_index("lat") * row_count + jnp.arange(row_count)
    polar_rows = (global_rows < PCAP) | (global_rows >= lat_total - PCAP)
    polar_mask = polar_rows[None, :, None, None, None]
    kernels = kernel_rows(spread, lon_count, reach)
    local_basis = circle_basis(lon_first, lon_count, lon_total)
    extended = extended_2(inputs, (("lat", 1),), 1, False)
    local_sums = jnp.einsum(
        "pj,erjc->eprc", local_basis, extended.astype(jnp.float32), precision=highest
    )
    circle_sums = lon_sum(local_sums)
    own = extended_2(inputs, (("lon", 2),), reach, True)
    edge_rows = jnp.concatenate([extended[:, :1], extended[:, row_count + 1 :]], 1)
    beyond = extended_2(edge_rows, (("lon", 2),), reach, True)

    def banded_row(row, lat_tap):
        source = row + lat_tap - 1
        if source < 0:
            strip = beyond[:, 0]
        elif source >= row_count:
            strip = beyond[:, 1]
        else:
            strip = own[:, source]
        return jnp.einsum(
            "bjq,eqc->ebjc", kernels[row], strip, preferred_element_type=jnp.float32
        )

    banded = jnp.stack(
        [
            jnp.concatenate([banded_row(row, lat_tap) for lat_tap in range(3)], 1)
            for row in range(row_count)
        ],
        1,
    )
    rounds = circular(circle_sums, local_basis, lon_total, row_count)
    features = jnp.where(polar_mask, rounds, banded).astype(jnp.bfloat16)
    lat_weight = jnp.sin(math.pi * (global_rows.astype(jnp.float32) + 0.5) / lat_total)
    scale = math.sqrt(weight.shape[0] * channels) / (lat_total * lon_total)
    if ens_local == 1 and fits(row_count, lon_count, channels, weight.shape[0]):
        wide = jnp.broadcast_to(lat_weight[:, None, None], (row_count, 1, channels))
        response, feature_grad, grad_weight, loss_parts = run_middle(
            scale, features[0], weight, target, wide
        )
        response, feature_grad = response[None], feature_grad[None]
        loss = jnp.sum(loss_parts[:, 0]) / (lat_total * lon_total * channels)
    else:
        response, feature_grad, grad_weight, loss = plain_middle(
            features, weight, target, lat_weight, scale, lat_total * lon_total * channels
        )
    band_kernels = jnp.where(polar_rows[:, None, None, None], 0.0, kernels).astype(jnp.bfloat16)
    high = local_basis.astype(jnp.bfloat16)
    low = (local_basis - high.astype(jnp.float32)).astype(jnp.bfloat16)
    waves = jnp.einsum(
        "pj,eokjc->eokpc",
        jnp.concatenate([high, low]),
        feature_grad,
        preferred_element_type=jnp.float32,
    )
    waves = waves[:, :, :, :3] + waves[:, :, :, 3:]
    waves = jnp.where(polar_mask, waves, 0.0)

    def circle_row(row, lat_tap):
        taps = waves[:, row, 3 * lat_tap : 3 * lat_tap + 3]
        mean_grad = taps[:, 0, 0] / lon_total
        cos_grad = 2.0 / lon_total * (taps[:, 1, 1] - taps[:, 2, 2])
        sin_grad = 2.0 / lon_total * (taps[:, 1, 2] + taps[:, 2, 1])
        return jnp.stack([mean_grad, cos_grad, sin_grad], 1)

    def band_row(row, lat_tap):
        return jnp.einsum(
            "bjq,ebjc->eqc",
            band_kernels[row],
            feature_grad[:, row, 3 * lat_tap : 3 * lat_tap + 3],
            preferred_element_type=jnp.float32,
        )

    last = row_count - 1
    down_window, up_window = lat_swap(
        band_row(0, 0).astype(jnp.bfloat16), band_row(last, 2).astype(jnp.bfloat16)
    )
    down_sums, up_sums = lat_swap(circle_row(0, 0), circle_row(last, 2))
    sum_rows, window_rows = [], []
    for source in range(row_count):
        pairs = [(row, source - row + 1) for row in range(row_count) if 0 <= source - row + 1 <= 2]
        sums = sum(circle_row(*pair) for pair in pairs)
        window = sum(band_row(*pair) for pair in pairs)
        if source == 0:
            sums, window = sums + up_sums, window + up_window.astype(jnp.float32)
        if source == last:
            sums, window = sums + down_sums, window + down_window.astype(jnp.float32)
        sum_rows.append(sums)
        window_rows.append(window)
    sum_total = lon_sum(jnp.stack(sum_rows, 2))
    window_grad = jnp.stack(window_rows, 1)
    circle_part = sum(
        local_basis[p][None, None, :, None] * sum_total[:, p][:, :, None, :] for p in range(3)
    )
    core = window_grad[:, :, reach : reach + lon_count] + circle_part
    rims = jnp.concatenate([window_grad[:, :, :reach], window_grad[:, :, reach + lon_count :]], 2)
    arrived = extended_2(rims.astype(jnp.bfloat16), (("lon", 2),), reach, True).astype(rims.dtype)
    core = jnp.concatenate(
        [
            core[:, :, :reach] + arrived[:, :, :reach],
            core[:, :, reach : lon_count - reach],
            core[:, :, lon_count - reach :] + arrived[:, :, 3 * reach :],
        ],
        2,
    )
    return (response, core.astype(jnp.bfloat16), grad_weight, loss)


def solution(mesh):
    in_specs = (P("ens", "lat", "lon", None), P(), P("lat"), P("lat", "lon", None))
    out_specs = (P("ens", "lat", "lon", None), P("ens", "lat", "lon", None), P(), P())
    return jax.shard_map(
        per_device, mesh=mesh, in_specs=in_specs, out_specs=out_specs, check_vma=False
    )
```

```python
import functools
import math

import jax
import jax.numpy as jnp
from jax import lax
from jax.experimental import pallas as pl
from jax.experimental.pallas import tpu as pltpu
from jax.sharding import PartitionSpec as P

PCAP = 2
HMAX = 16


highest = lax.Precision.HIGHEST


def extended_2(block, sides, width, periodic):
    for axis, dim in sides:
        count = lax.axis_size(axis)
        forward = [(i, i + 1) for i in range(count - 1)]
        if periodic:
            forward.append((count - 1, 0))
        backward = [(target, source) for source, target in forward]
        low = lax.ppermute(
            lax.slice_in_dim(block, block.shape[dim] - width, None, axis=dim), axis, forward
        )
        high = lax.ppermute(lax.slice_in_dim(block, 0, width, axis=dim), axis, backward)
        block = jnp.concatenate([low, block, high], axis=dim)
    return block


def kernel_rows(spread_rows, lon_count, reach):
    halves = spread_rows.astype(jnp.float32)[:, None, None, None] / 2.0
    columns = jnp.arange(lon_count)
    window_cols = jnp.arange(lon_count + 2 * reach)
    offsets = (window_cols[None, :] - reach - columns[:, None]).astype(jnp.float32)
    centres = (jnp.arange(3) - 1).astype(jnp.float32)[None, :, None, None] * halves
    values = jnp.maximum(0.0, 1.0 - jnp.abs(offsets[None, None] - centres) / halves) / halves
    return values.astype(jnp.bfloat16)


def circle_basis(first_col, lon_count, circle):
    angles = 2.0 * math.pi * (first_col + jnp.arange(lon_count)).astype(jnp.float32) / circle
    return jnp.stack([jnp.ones_like(angles), jnp.cos(angles), jnp.sin(angles)])


def circular(circle_sums, basis, circle, row_count):
    cos_wave = basis[1][None, None, :, None]
    sin_wave = basis[2][None, None, :, None]
    pieces = []
    for lat_tap in range(3):
        tap_sums = circle_sums[:, :, lat_tap : lat_tap + row_count]
        mean_part = tap_sums[:, 0][:, :, None, :] / circle
        cosine_part = (
            2.0
            / circle
            * (cos_wave * tap_sums[:, 1][:, :, None, :] + sin_wave * tap_sums[:, 2][:, :, None, :])
        )
        sine_part = (
            2.0
            / circle
            * (cos_wave * tap_sums[:, 2][:, :, None, :] - sin_wave * tap_sums[:, 1][:, :, None, :])
        )
        pieces += [jnp.broadcast_to(mean_part, cosine_part.shape), cosine_part, sine_part]
    return jnp.stack(pieces, 2)


def crps_terms(values, every_member, truth, lat_weight, member_total):
    miss = values - truth
    own_dist = jnp.sqrt(miss * miss + 0.25)
    own_slope = miss / own_dist

    def add_member(member, carry):
        pair_dist, pair_slope = carry
        other = lax.dynamic_index_in_dim(every_member, member, 0, keepdims=True).astype(jnp.float32)
        gap_value = values - other
        distance = jnp.sqrt(gap_value * gap_value + 0.25)
        return (pair_dist + distance, pair_slope + gap_value / distance)

    start = (jnp.zeros_like(values), jnp.zeros_like(values))
    pair_dist, pair_slope = lax.fori_loop(0, member_total, add_member, start)
    pair_dist = pair_dist - 0.5
    scores = own_dist / member_total - pair_dist / (2 * member_total * (member_total - 1))
    weighted = jnp.sum(lat_weight * scores)
    slopes = (
        lat_weight * (own_slope / member_total - pair_slope / (member_total * (member_total - 1)))
    ).astype(jnp.bfloat16)
    return (weighted, slopes)


MESH = pl.DeviceIdType.MESH
ROWDOT = (((0,), (0,)), ((), ()))
COLDOT = (((1,), (1,)), ((), ()))


def pick_tile(lon_count):
    for tile in (240, 80):
        if lon_count % tile == 0:
            return tile
    return 0


def fits(row_count, lon_count, channels, taps):
    lats, lons, members = (lax.axis_size(a) for a in ("lat", "lon", "ens"))
    return (
        lons == 2
        and members <= 8
        and lats <= 8
        and channels % 256 == 0
        and pick_tile(lon_count) > 0
        and (taps * channels) % (16 * lats * members) == 0
    )


def middle(scale, feat, weight, target, row_weight, resp, fg, grad_w, loss, rsp, gath, acc, losses,
           send1, recv1, given, send4, recv4, score_sum, slopes, out2, in2, red2, out3, in3, red3, full, sems, loss_sems):
    members, lats = lax.axis_size("ens"), lax.axis_size("lat")
    me, my_lat, my_lon = lax.axis_index("ens"), lax.axis_index("lat"), lax.axis_index("lon")
    rows, taps, lon_count, channels = feat.shape
    tile = pick_tile(lon_count)
    per_row = lon_count // tile
    chunks = rows * per_row
    half = channels // 2

    def peer(axis, here, count, step):
        return {axis: lax.rem(here + step, count)}

    barrier = pltpu.get_barrier_semaphore()
    peers = (
        [peer("ens", me, members, p) for p in range(1, members)]
        + [peer("lat", my_lat, lats, p) for p in range(1, lats)]
        + [{"lon": 1 - my_lon}]
    )
    for other in peers:
        pl.semaphore_signal(barrier, inc=1, device_id=other, device_id_type=MESH)
    pl.semaphore_wait(barrier, len(peers))

    def where(i):
        return i // per_row, pl.ds(pl.multiple_of(lax.rem(i, per_row) * tile, 16), tile)

    subs = 5
    sub = tile // subs

    def cell(t):
        i = t // subs
        first = lax.rem(i, per_row) * tile + lax.rem(t, subs) * sub
        return i // per_row, pl.ds(pl.multiple_of(first, 16), sub), lax.rem(t, members)

    def to_owner(t):
        o, cols, owner = cell(t)
        slot = lax.rem(owner - me + members, members) - 1
        return pltpu.make_async_remote_copy(
            src_ref=rsp.at[o, cols], dst_ref=gath.at[slot, o, cols],
            send_sem=send1.at[0, t], recv_sem=recv1.at[slot, t],
            device_id={"ens": owner}, device_id_type=MESH,
        )

    def from_member(t, p):
        o, cols, owner = cell(t)
        return pltpu.make_async_remote_copy(
            src_ref=rsp.at[o, cols], dst_ref=gath.at[p - 1, o, cols],
            send_sem=send1.at[0, t], recv_sem=recv1.at[p - 1, t],
            device_id=peer("ens", me, members, p), device_id_type=MESH,
        )

    def to_member(t, p):
        o, cols, owner = cell(t)
        return pltpu.make_async_remote_copy(
            src_ref=given.at[p - 1, o, cols], dst_ref=slopes.at[o, cols],
            send_sem=send4.at[p - 1, t], recv_sem=recv4.at[t],
            device_id=peer("ens", me, members, members - p), device_id_type=MESH,
        )

    def forward(i, carry):
        o, cols = where(i)
        total = jnp.zeros((tile, channels), jnp.float32)
        for k in range(taps):
            total = total + jnp.dot(feat[o, k, cols], weight[k], preferred_element_type=jnp.float32)
        rsp[o, cols] = total.astype(jnp.bfloat16)
        for u in range(subs):
            t = i * subs + u

            @pl.when(lax.rem(t, members) != me)
            def _():
                to_owner(t).start()

        return carry

    lax.fori_loop(0, chunks, forward, 0)
    score_sum[...] = jnp.zeros_like(score_sum)
    resp[...] = rsp[...]
    acc[...] = jnp.zeros_like(acc)

    def crps(t, carry):
        o, cols, owner = cell(t)

        @pl.when(owner == me)
        def _():
            for p in range(1, members):
                from_member(t, p).wait_recv()
            values = [rsp[o, cols].astype(jnp.float32)]
            values += [gath[p - 1, o, cols].astype(jnp.float32) for p in range(1, members)]
            truth = target[o, cols].astype(jnp.float32)
            own_dist = jnp.zeros_like(truth)
            pair_dist = jnp.zeros_like(truth)
            own_slopes, pair_slopes = [], [jnp.zeros_like(truth) for _ in values]
            for value in values:
                miss = value - truth
                square = miss * miss + 0.25
                inverse = lax.rsqrt(square)
                own_dist = own_dist + square * inverse
                own_slopes.append(miss * inverse)
            for m in range(members):
                for n in range(m):
                    gap = values[m] - values[n]
                    square = gap * gap + 0.25
                    inverse = lax.rsqrt(square)
                    pair_dist = pair_dist + square * inverse
                    tilt = gap * inverse
                    pair_slopes[m] = pair_slopes[m] + tilt
                    pair_slopes[n] = pair_slopes[n] - tilt
            lat_weight = row_weight[o]
            for p in range(members):
                slope = lat_weight * (
                    own_slopes[p] / members - pair_slopes[p] / (members * (members - 1))
                )
                if p == 0:
                    slopes[o, cols] = slope.astype(jnp.bfloat16)
                else:
                    given[p - 1, o, cols] = slope.astype(jnp.bfloat16)
                    to_member(t, p).start()
            score = own_dist / members - pair_dist / (members * (members - 1))
            score_sum[...] += lat_weight * jnp.sum(score.reshape(sub // 8, 8, channels), axis=0)

        return carry

    lax.fori_loop(0, chunks * subs, crps, 0)

    def backward(i, carry):
        o, cols = where(i)
        for u in range(subs):
            t = i * subs + u

            @pl.when(lax.rem(t, members) != me)
            def _():
                to_member(t, 1).wait_recv()

        slope = slopes[o, cols]
        for k in range(taps):
            part = lax.dot_general(feat[o, k, cols], slope, ROWDOT, preferred_element_type=jnp.float32)
            for h in range(2):
                acc[h, pl.ds(k * channels, channels)] += part[:, h * half : (h + 1) * half]
        return carry

    stages = 6

    def beside(stage):
        def spread_back(i, carry):
            o, cols = where(i)
            for k in range(taps):
                fg[o, k, cols] = lax.dot_general(
                    slopes[o, cols], weight[k], COLDOT, preferred_element_type=jnp.float32
                ).astype(jnp.bfloat16)
            return carry

        lax.fori_loop(chunks * stage // stages, chunks * (stage + 1) // stages, spread_back, 0)

    lax.fori_loop(0, chunks, backward, 0)
    score = score_sum[...]
    part_loss = jnp.sum(score, axis=1, keepdims=True) * jnp.ones((8, 128), jnp.float32)

    def remote(src, dst, at, other):
        return pltpu.make_async_remote_copy(
            src_ref=src, dst_ref=dst, send_sem=sems.at[0, at], recv_sem=sems.at[1, at],
            device_id=other, device_id_type=MESH,
        )

    def remote_loss(src, dst, at, other):
        return pltpu.make_async_remote_copy(
            src_ref=src, dst_ref=dst, send_sem=loss_sems.at[0, at], recv_sem=loss_sems.at[1, at],
            device_id=other, device_id_type=MESH,
        )

    def finish(copies):
        for copy in copies:
            copy.wait_recv()

    pending = []
    at, lat_at = 0, 0
    out2[...] = acc[1 - my_lon].astype(jnp.bfloat16).reshape(out2.shape)
    losses[0] = part_loss
    copies = [
        remote(out2, in2, at, {"lon": 1 - my_lon}),
        remote_loss(losses.at[0], losses.at[1], lat_at, {"lon": 1 - my_lon}),
    ]
    for copy in copies:
        copy.start()
    beside(0)
    finish(copies)
    pending += copies
    at, lat_at = at + 1, lat_at + 1
    red2[...] = acc[my_lon].reshape(red2.shape) + in2[...].astype(jnp.float32)
    base = 2
    losses[base + my_lat] = losses[0] + losses[1]
    send2 = out3
    send2[...] = red2[...].astype(jnp.bfloat16)
    copies = []
    for p in range(1, lats):
        other = peer("lat", my_lat, lats, p)
        copies.append(remote(send2.at[other["lat"]], in3.at[p - 1], at, other))
        copies.append(remote_loss(losses.at[base + my_lat], losses.at[base + my_lat], lat_at, other))
        at, lat_at = at + 1, lat_at + 1
    for copy in copies:
        copy.start()
    beside(1)
    finish(copies)
    pending += copies
    total = red2[my_lat]
    for p in range(1, lats):
        total = total + in3[p - 1].astype(jnp.float32)
    parts = red3.shape[0]
    red3[...] = total.reshape(parts, total.shape[0] // parts, half)
    total = losses[base]
    for p in range(1, lats):
        total = total + losses[base + p]
    base = base + lats
    losses[base + me] = total
    red_out, red_in = full_split(full, members)
    red_out[...] = red3[...].astype(jnp.bfloat16)
    copies = []
    for p in range(1, members):
        other = peer("ens", me, members, p)
        copies.append(remote(red_out.at[other["ens"]], red_in.at[p - 1], at, other))
        copies.append(remote_loss(losses.at[base + me], losses.at[base + me], lat_at, other))
        at, lat_at = at + 1, lat_at + 1
    for copy in copies:
        copy.start()
    beside(2)
    finish(copies)
    pending += copies
    total = red3[me]
    for p in range(1, members):
        total = total + red_in[p - 1].astype(jnp.float32)
    gathered = full[2]
    gathered[my_lon, my_lat, me] = (total * scale).astype(jnp.bfloat16)
    total = losses[base]
    for p in range(1, members):
        total = total + losses[base + p]
    loss[...] = total
    mine = gathered.at[my_lon, my_lat, me]
    copies = []
    for p in range(1, members):
        copies.append(remote(mine, mine, at, peer("ens", me, members, p)))
        at += 1
    for copy in copies:
        copy.start()
    beside(3)
    finish(copies)
    pending += copies
    mine = gathered.at[my_lon, my_lat]
    copies = []
    for p in range(1, lats):
        copies.append(remote(mine, mine, at, peer("lat", my_lat, lats, p)))
        at += 1
    for copy in copies:
        copy.start()
    beside(4)
    finish(copies)
    pending += copies
    mine = gathered.at[my_lon]
    copies = [remote(mine, mine, at, {"lon": 1 - my_lon})]
    copies[0].start()
    beside(5)
    finish(copies)
    pending += copies
    for h in range(2):
        grad_w[:, :, h * half : (h + 1) * half] = (
            gathered[h].astype(jnp.float32).reshape(taps, channels, half)
        )
    for copy in pending:
        copy.wait_send()

    def drain(t, carry):
        @pl.when(lax.rem(t, members) != me)
        def _():
            to_owner(t).wait_send()

        @pl.when(lax.rem(t, members) == me)
        def _():
            for p in range(1, members):
                to_member(t, p).wait_send()

        return carry

    lax.fori_loop(0, chunks * subs, drain, 0)


def full_split(full, members):
    return full[0], full[1]


def run_middle(scale, feat, weight, target, row_weight):
    members, lats = lax.axis_size("ens"), lax.axis_size("lat")
    rows, taps, lon_count, channels = feat.shape
    chunks = rows * (lon_count // pick_tile(lon_count))
    half = channels // 2
    flat = taps * channels
    band, piece = flat // lats, flat // lats // members
    bf16, f32 = jnp.bfloat16, jnp.float32
    shape = jax.ShapeDtypeStruct
    whole = pl.BlockSpec(memory_space=pltpu.VMEM)
    count = 1 + 2 * (lats - 1) + 2 * (members - 1) + 1
    loss_count = 1 + (lats - 1) + (members - 1)
    return pl.pallas_call(
        functools.partial(middle, scale),
        out_shape=[
            shape((rows, lon_count, channels), bf16),
            shape(feat.shape, bf16),
            shape((taps, channels, channels), f32),
            shape((8, 128), f32),
        ],
        in_specs=[whole] * 4,
        out_specs=[whole] * 4,
        scratch_shapes=[
            pltpu.VMEM((rows, lon_count, channels), bf16),
            pltpu.VMEM((members - 1, rows, lon_count, channels), bf16),
            pltpu.VMEM((2, flat, half), f32),
            pltpu.VMEM((2 + lats + members, 8, 128), f32),
            pltpu.SemaphoreType.DMA((1, 5 * chunks)),
            pltpu.SemaphoreType.DMA((members - 1, 5 * chunks)),
            pltpu.VMEM((members - 1, rows, lon_count, channels), bf16),
            pltpu.SemaphoreType.DMA((members - 1, 5 * chunks)),
            pltpu.SemaphoreType.DMA((5 * chunks,)),
            pltpu.VMEM((8, channels), f32),
            pltpu.VMEM((rows, lon_count, channels), bf16),
            pltpu.VMEM((lats, band, half), bf16),
            pltpu.VMEM((lats, band, half), bf16),
            pltpu.VMEM((lats, band, half), f32),
            pltpu.VMEM((lats, band, half), bf16),
            pltpu.VMEM((lats - 1, band, half), bf16),
            pltpu.VMEM((members, piece, half), f32),
            [
                pltpu.VMEM((members, piece, half), bf16),
                pltpu.VMEM((members - 1, piece, half), bf16),
                pltpu.VMEM((2, lats, members, piece, half), bf16),
            ],
            pltpu.SemaphoreType.DMA((2, count)),
            pltpu.SemaphoreType.DMA((2, loss_count)),
        ],
        compiler_params=pltpu.CompilerParams(
            collective_id=0, has_side_effects=True, vmem_limit_bytes=50 * 1024 * 1024
        ),
        name="middle",
    )(feat, weight, target, row_weight)


def plain_middle(features, weight, target, row_weight, scale, cells):
    response = jnp.einsum(
        "eokjc,kcd->eojd", features, weight, preferred_element_type=jnp.float32
    ).astype(jnp.bfloat16)
    member_total = features.shape[0] * lax.axis_size("ens")
    ensemble = lax.all_gather(response, "ens", axis=0, tiled=True)
    truth = target.astype(jnp.float32)[None]
    weighted, slopes = crps_terms(
        response.astype(jnp.float32), ensemble, truth, row_weight[None, :, None, None], member_total
    )
    loss_part = weighted / cells
    weight_part = jnp.einsum(
        "eokjc,eojd->kcd", features, slopes, preferred_element_type=jnp.float32
    )
    weight_sum, loss = lax.psum((weight_part, loss_part), ("lat", "lon", "ens"))
    feature_grad = jnp.einsum(
        "eojd,kcd->eokjc", slopes, weight, preferred_element_type=jnp.float32
    ).astype(jnp.bfloat16)
    return response, feature_grad, weight_sum * scale, loss


def lon_sum(value):
    if lax.axis_size("lon") == 2:
        return value + lax.ppermute(value, "lon", [(0, 1), (1, 0)])
    return lax.psum(value, "lon")


def lat_swap(down, up):
    count = lax.axis_size("lat")
    forward = [(i, i + 1) for i in range(count - 1)]
    backward = [(target, source) for source, target in forward]
    return lax.ppermute(down, "lat", backward), lax.ppermute(up, "lat", forward)


def per_device(inputs, weight, spread, target):
    ens_local, row_count, lon_count, channels = inputs.shape
    reach = HMAX
    lat_total = row_count * lax.axis_size("lat")
    lon_total = lon_count * lax.axis_size("lon")
    lon_first = lax.axis_index("lon") * lon_count
    global_rows = lax.axis_index("lat") * row_count + jnp.arange(row_count)
    polar_rows = (global_rows < PCAP) | (global_rows >= lat_total - PCAP)
    polar_mask = polar_rows[None, :, None, None, None]
    kernels = kernel_rows(spread, lon_count, reach)
    local_basis = circle_basis(lon_first, lon_count, lon_total)
    extended = extended_2(inputs, (("lat", 1),), 1, False)
    local_sums = jnp.einsum(
        "pj,erjc->eprc", local_basis, extended.astype(jnp.float32), precision=highest
    )
    circle_sums = lon_sum(local_sums)
    own = extended_2(inputs, (("lon", 2),), reach, True)
    edge_rows = jnp.concatenate([extended[:, :1], extended[:, row_count + 1 :]], 1)
    beyond = extended_2(edge_rows, (("lon", 2),), reach, True)

    def banded_row(row, lat_tap):
        source = row + lat_tap - 1
        if source < 0:
            strip = beyond[:, 0]
        elif source >= row_count:
            strip = beyond[:, 1]
        else:
            strip = own[:, source]
        return jnp.einsum(
            "bjq,eqc->ebjc", kernels[row], strip, preferred_element_type=jnp.float32
        )

    banded = jnp.stack(
        [
            jnp.concatenate([banded_row(row, lat_tap) for lat_tap in range(3)], 1)
            for row in range(row_count)
        ],
        1,
    )
    rounds = circular(circle_sums, local_basis, lon_total, row_count)
    features = jnp.where(polar_mask, rounds, banded).astype(jnp.bfloat16)
    lat_weight = jnp.sin(math.pi * (global_rows.astype(jnp.float32) + 0.5) / lat_total)
    scale = math.sqrt(weight.shape[0] * channels) / (lat_total * lon_total)
    if ens_local == 1 and fits(row_count, lon_count, channels, weight.shape[0]):
        wide = jnp.broadcast_to(lat_weight[:, None, None], (row_count, 1, channels))
        response, feature_grad, grad_weight, loss_parts = run_middle(
            scale, features[0], weight, target, wide
        )
        response, feature_grad = response[None], feature_grad[None]
        loss = jnp.sum(loss_parts[:, 0]) / (lat_total * lon_total * channels)
    else:
        response, feature_grad, grad_weight, loss = plain_middle(
            features, weight, target, lat_weight, scale, lat_total * lon_total * channels
        )
    band_kernels = jnp.where(polar_rows[:, None, None, None], 0.0, kernels).astype(jnp.bfloat16)
    high = local_basis.astype(jnp.bfloat16)
    low = (local_basis - high.astype(jnp.float32)).astype(jnp.bfloat16)
    waves = jnp.einsum(
        "pj,eokjc->eokpc",
        jnp.concatenate([high, low]),
        feature_grad,
        preferred_element_type=jnp.float32,
    )
    waves = waves[:, :, :, :3] + waves[:, :, :, 3:]
    waves = jnp.where(polar_mask, waves, 0.0)

    def circle_row(row, lat_tap):
        taps = waves[:, row, 3 * lat_tap : 3 * lat_tap + 3]
        mean_grad = taps[:, 0, 0] / lon_total
        cos_grad = 2.0 / lon_total * (taps[:, 1, 1] - taps[:, 2, 2])
        sin_grad = 2.0 / lon_total * (taps[:, 1, 2] + taps[:, 2, 1])
        return jnp.stack([mean_grad, cos_grad, sin_grad], 1)

    def band_row(row, lat_tap):
        return jnp.einsum(
            "bjq,ebjc->eqc",
            band_kernels[row],
            feature_grad[:, row, 3 * lat_tap : 3 * lat_tap + 3],
            preferred_element_type=jnp.float32,
        )

    last = row_count - 1
    down_window, up_window = lat_swap(
        band_row(0, 0).astype(jnp.bfloat16), band_row(last, 2).astype(jnp.bfloat16)
    )
    down_sums, up_sums = lat_swap(circle_row(0, 0), circle_row(last, 2))
    sum_rows, window_rows = [], []
    for source in range(row_count):
        pairs = [(row, source - row + 1) for row in range(row_count) if 0 <= source - row + 1 <= 2]
        sums = sum(circle_row(*pair) for pair in pairs)
        window = sum(band_row(*pair) for pair in pairs)
        if source == 0:
            sums, window = sums + up_sums, window + up_window.astype(jnp.float32)
        if source == last:
            sums, window = sums + down_sums, window + down_window.astype(jnp.float32)
        sum_rows.append(sums)
        window_rows.append(window)
    sum_total = lon_sum(jnp.stack(sum_rows, 2))
    window_grad = jnp.stack(window_rows, 1)
    circle_part = sum(
        local_basis[p][None, None, :, None] * sum_total[:, p][:, :, None, :] for p in range(3)
    )
    core = window_grad[:, :, reach : reach + lon_count] + circle_part
    rims = jnp.concatenate([window_grad[:, :, :reach], window_grad[:, :, reach + lon_count :]], 2)
    arrived = extended_2(rims.astype(jnp.bfloat16), (("lon", 2),), reach, True).astype(rims.dtype)
    core = jnp.concatenate(
        [
            core[:, :, :reach] + arrived[:, :, :reach],
            core[:, :, reach : lon_count - reach],
            core[:, :, lon_count - reach :] + arrived[:, :, 3 * reach :],
        ],
        2,
    )
    return (response, core.astype(jnp.bfloat16), grad_weight, loss)


def solution(mesh):
    in_specs = (P("ens", "lat", "lon", None), P(), P("lat"), P("lat", "lon", None))
    out_specs = (P("ens", "lat", "lon", None), P("ens", "lat", "lon", None), P(), P())
    return jax.shard_map(
        per_device, mesh=mesh, in_specs=in_specs, out_specs=out_specs, check_vma=False
    )
```
